32 devices in a mesh: grp: 2 (over x), col: 16 (over z, y, core).
Axes of the slice: x: 2, y: 2, z: 4, core: 2. Of those that a mesh axis runs over, the one named last changes fastest.
Arguments:
- adjoint_in: bfloat16 [768, 137, 128], P(('grp', 'col')), parts along dimension 0, may hold values from -6 to 6
- vertical: bfloat16 [768, 137, 137], P(('grp', 'col')), parts along dimension 0, may hold values from -0.5 to 0.5
- tiles: bfloat16 [768, 8, 128, 128], P(('grp', 'col')), parts along dimension 0, may hold values from -0.5 to 0.5
- sources: int32 [768, 8], P(('grp', 'col')), parts along dimension 0, may hold values from 0 to 383, as said below
- lengths: int32 [768], P(('grp', 'col')), parts along dimension 0, may hold values from 1 to 8, as said below
- prior: float32 [768, 137, 128], P(('grp', 'col')), parts along dimension 0, may hold values from -6 to 6
Outputs:
- adjoint_out: float32 [768, 137, 128], P(('grp', 'col')), parts along dimension 0
The draws below stay inside these ranges and needn't reach their ends.
There are 2 independent parts, one for each index of `grp`. The reference program is written for one: setup_inputs(seed, part) draws one part's arguments, and reference() takes and returns one part's arrays. A program takes and returns all parts, laid end to end along the dimension named above; each array names one. Nothing has to cross between parts.
Inputs may be any that keep to these rules, and one draw needn't show every extreme that they name: `sources`: each entry lies within 24 blocks of its arrival block, counted cyclically over the 384 blocks; some entry lies exactly 24 blocks ahead and some exactly 24 blocks behind. `lengths`: A run of 48 cyclically consecutive blocks has full lists.
All inputs are finite; a program needn't handle non-finite values.
Results may differ from the reference program's by a relative error of at most 0.0026.
Values may be sent and summed in bfloat16 or wider, within the bound.
A program may use at most 128 MiB of HBM per device.

```python
import jax
import jax.numpy as jnp
from jax import lax

L = 137
B = 128
KMAX = 8
BLK_DEV = 24
BLOCKS = 384


def draw_sources(key, part):
    key = jax.random.fold_in(key, 23)
    key_one, key_two, key_three = jax.random.split(key, 3)
    shifts = jax.random.randint(key_one, (BLOCKS, KMAX), -BLK_DEV, BLK_DEV + 1)
    spot_ahead = jax.random.randint(key_two, (), 0, BLOCKS)
    spot_behind = (spot_ahead + 1 + jax.random.randint(key_three, (), 0, BLOCKS - 1)) % BLOCKS
    shifts = shifts.at[spot_ahead, 0].set(BLK_DEV)
    shifts = shifts.at[spot_behind, 0].set(-BLK_DEV)
    position = jnp.arange(BLOCKS, dtype=jnp.int32)[:, None]
    return ((position + shifts) % BLOCKS).astype(jnp.int32)


def draw_lengths(key, part):
    key = jax.random.fold_in(key, 11)
    key_one, key_two, key_three = jax.random.split(key, 3)
    first_draw = jax.random.randint(key_one, (BLOCKS,), 1, KMAX + 1)
    second_draw = jax.random.randint(key_two, (BLOCKS,), 1, KMAX + 1)
    jet_start = jax.random.randint(key_three, (), 0, BLOCKS)
    position = jnp.arange(BLOCKS, dtype=jnp.int32)
    in_jet = (position - jet_start) % BLOCKS < 2 * BLK_DEV
    return jnp.where(in_jet, KMAX, jnp.minimum(first_draw, second_draw)).astype(jnp.int32)


def level_of(stream_key, dims, cuts, least, top_value):
    gain, own = 1.0, jax.random.fold_in(stream_key, 6)
    for dim, parts in cuts:
        draws = jnp.exp(jax.random.uniform(jax.random.fold_in(own, dim), (parts,), jnp.float32, least / len(cuts), top_value / len(cuts)))
        gain = gain * jnp.repeat(draws, dims[dim] // parts).reshape([-1 if axis == dim else 1 for axis in range(len(dims))])
    return gain


def noise(own_key, dims, scale, most, cuts=(), kind=jnp.bfloat16):
    result = scale * jax.random.normal(own_key, dims, jnp.float32)
    if cuts:
        result = result * level_of(own_key, dims, cuts, -0.22, 0.18)
    return jnp.clip(result, -most, most).astype(kind)


def setup_inputs(seed: int = 0, part: int = 0) -> dict:
    key_list = jax.random.split(jax.random.key(seed), 7)
    part_splits = jax.random.split(jax.random.fold_in(key_list[6], part), 7)
    adjoint_in = noise(part_splits[0], (BLOCKS, L, B), 1.0, 6.0, ((0, 16),))
    vertical = noise(part_splits[1], (BLOCKS, L, L), L ** -0.5, 0.5, ((0, 16),))
    tiles = noise(part_splits[2], (BLOCKS, KMAX, B, B), B ** -0.5, 0.5, ((0, 16),))
    sources = draw_sources(jax.random.fold_in(jax.random.fold_in(key_list[6], part), 71), part)
    lengths = draw_lengths(jax.random.fold_in(jax.random.fold_in(key_list[6], part), 71), part)
    prior = noise(part_splits[5], (BLOCKS, L, B), 1.0, 6.0, ((0, 16),), jnp.float32)
    return dict(adjoint_in=adjoint_in, vertical=vertical, tiles=tiles, sources=sources, lengths=lengths, prior=prior)


def reference(adjoint_in, vertical, tiles, sources, lengths, prior):
    lifted = jnp.einsum("tml,tmb->tlb", vertical.astype(jnp.float32), adjoint_in.astype(jnp.float32)).astype(jnp.bfloat16)
    live = jnp.arange(KMAX, dtype=jnp.int32)[None, :] < lengths[:, None]

    def visit(running, flat_index):
        block = (flat_index // KMAX).astype(jnp.int32)
        entry = (flat_index % KMAX).astype(jnp.int32)
        product = jnp.dot(lifted[block], tiles[block, entry], preferred_element_type=jnp.float32)
        product = jnp.where(live[block, entry], product, jnp.zeros_like(product))
        target = sources[block, entry].astype(jnp.int32)
        before = lax.dynamic_index_in_dim(running, target, 0, keepdims=False)
        running = lax.dynamic_update_index_in_dim(running, before + product, target, 0)
        return running, None

    running, _ = lax.scan(visit, prior, jnp.arange(BLOCKS * KMAX, dtype=jnp.int32))
    return running
```

```python
import functools

import jax
import jax.numpy as jnp
from jax import lax
from jax.experimental import pallas as pl
from jax.experimental.pallas import tpu as pltpu
from jax.sharding import PartitionSpec as P

GROUP = 8
VMEM_BYTES = 48 << 20


def relative(source, first, blocks, everywhere):
    rel = source - first
    rel = jnp.where(rel < -blocks, rel + everywhere, rel)
    return jnp.where(rel >= 2 * blocks, rel - everywhere, rel)


def make_list(pick, trash, axis, src_ref, len_ref, entry_list, slot_list):
    blocks, listed = src_ref.shape
    everywhere = lax.axis_size(axis) * blocks
    first = lax.axis_index(axis) * blocks

    def visit(t, count):
        length = len_ref[t]
        for k in range(listed):
            rel = relative(src_ref[t, k], first, blocks, everywhere)
            keep, slot = pick(rel)
            keep = jnp.logical_and(keep, k < length)
            entry_list[count] = t * listed + k
            slot_list[count] = slot
            count = count + keep.astype(jnp.int32)
        return count

    count = lax.fori_loop(0, blocks, visit, jnp.int32(0))
    for extra in range(GROUP):
        entry_list[count + extra] = 0
        slot_list[count + extra] = trash
    return count


def add_products(count, listed, entry_list, slot_list, lifted, tiles, running):
    def group(g, carry):
        for u in range(GROUP):
            entry = entry_list[g * GROUP + u]
            slot = slot_list[g * GROUP + u]
            product = jnp.dot(
                lifted[lax.div(entry, listed)], tiles[entry], preferred_element_type=jnp.float32
            )
            running[slot] += product
        return carry

    lax.fori_loop(0, lax.div(count + (GROUP - 1), GROUP), group, 0)


def fetch_tiles(tiles_hbm, tiles, sems, parts):
    each = tiles.shape[0] // parts
    copies = []
    for part in range(parts):
        rows = pl.ds(part * each, each)
        copies.append(pltpu.make_async_copy(tiles_hbm.at[rows], tiles.at[rows], sems.at[part]))
    return copies


def pick_rim(blocks, low, up, rel):
    low_from, low_to = low
    up_from, up_to = up
    is_low = jnp.logical_and(rel >= low_from - blocks, rel < low_to - blocks)
    is_up = jnp.logical_and(rel >= up_from + blocks, rel < up_to + blocks)
    slot = jnp.where(is_low, rel + (blocks - low_from), rel - (blocks + up_from) + (low_to - low_from))
    return jnp.logical_or(is_low, is_up), slot


def emit_rims(low_count, up_count, running, low_ref, up_ref):
    def low_body(j, carry):
        low_ref[j] = running[j].astype(low_ref.dtype)
        return carry

    def up_body(j, carry):
        up_ref[j] = running[low_count + j].astype(up_ref.dtype)
        return carry

    lax.fori_loop(0, low_count, low_body, 0)
    lax.fori_loop(0, up_count, up_body, 0)


def clear(running):
    def body(j, carry):
        running[j] = jnp.zeros_like(running[j])
        return carry

    lax.fori_loop(0, running.shape[0], body, 0)


def early_kernel(axis, low, up, parts, src_ref, len_ref, a_hbm, v_hbm, tiles_hbm, low_ref, up_ref, lifted,
                 a, v, tiles, running, entry_list, slot_list, sems, tile_sems):
    blocks, listed = src_ref.shape
    copy_a = pltpu.make_async_copy(a_hbm, a, sems.at[0])
    copy_v = pltpu.make_async_copy(v_hbm, v, sems.at[1])
    copy_v.start()
    copy_a.start()
    copies = fetch_tiles(tiles_hbm, tiles, tile_sems, parts)
    for copy in copies:
        copy.start()
    trash = running.shape[0] - 1
    count = make_list(functools.partial(pick_rim, blocks, low, up), trash, axis, src_ref, len_ref, entry_list, slot_list)
    clear(running)
    copy_v.wait()
    copy_a.wait()

    def lift(i, carry):
        for u in range(4):
            t = i * 4 + u
            lifted[t] = lax.dot_general(
                v[t], a[t], (((0,), (0,)), ((), ())), preferred_element_type=jnp.float32
            ).astype(lifted.dtype)
        return carry

    lax.fori_loop(0, blocks // 4, lift, 0)
    for copy in copies:
        copy.wait()
    add_products(count, listed, entry_list, slot_list, lifted, tiles, running)
    emit_rims(low[1] - low[0], up[1] - up[0], running, low_ref, up_ref)


def late_kernel(axis, low, up, parts, src_ref, len_ref, lifted, tiles_hbm, low_ref, up_ref,
                tiles, running, entry_list, slot_list, tile_sems):
    blocks, listed = src_ref.shape
    copies = fetch_tiles(tiles_hbm, tiles, tile_sems, parts)
    for copy in copies:
        copy.start()
    trash = running.shape[0] - 1
    count = make_list(functools.partial(pick_rim, blocks, low, up), trash, axis, src_ref, len_ref, entry_list, slot_list)
    clear(running)
    for copy in copies:
        copy.wait()
    add_products(count, listed, entry_list, slot_list, lifted, tiles, running)
    emit_rims(low[1] - low[0], up[1] - up[0], running, low_ref, up_ref)


def middle_kernel(axis, parts, low_from, up_from, src_ref, len_ref, lifted, tiles_hbm, prior_hbm, low_hbm, up_hbm, out_hbm,
                  tiles, running, low_got, up_got, entry_list, slot_list, sems, tile_sems):
    blocks, listed = src_ref.shape
    kept = running.at[pl.ds(0, blocks)]
    copy_prior = pltpu.make_async_copy(prior_hbm, kept, sems.at[0])
    copy_low = pltpu.make_async_copy(low_hbm, low_got, sems.at[1])
    copy_up = pltpu.make_async_copy(up_hbm, up_got, sems.at[2])
    copy_prior.start()
    copy_low.start()
    copy_up.start()
    copies = fetch_tiles(tiles_hbm, tiles, tile_sems, parts)
    for copy in copies:
        copy.start()

    def pick(rel):
        return jnp.logical_and(rel >= 0, rel < blocks), rel

    running[blocks] = jnp.zeros_like(running[blocks])
    count = make_list(pick, blocks, axis, src_ref, len_ref, entry_list, slot_list)
    copy_prior.wait()
    copy_low.wait()
    copy_up.wait()

    def add_low(j, carry):
        running[low_from + j] += low_got[j].astype(jnp.float32)
        return carry

    def add_up(j, carry):
        running[up_from + j] += up_got[j].astype(jnp.float32)
        return carry

    lax.fori_loop(0, low_got.shape[0], add_low, 0)
    lax.fori_loop(0, up_got.shape[0], add_up, 0)
    for copy in copies:
        copy.wait()
    add_products(count, listed, entry_list, slot_list, lifted, tiles, running)
    copy_out = pltpu.make_async_copy(kept, out_hbm, sems.at[3])
    copy_out.start()
    copy_out.wait()


SMEM = pl.BlockSpec(memory_space=pltpu.SMEM)
VMEM = pl.BlockSpec(memory_space=pltpu.VMEM)
HBM = pl.BlockSpec(memory_space=pl.ANY)


def shift(value, axis, steps):
    count = lax.axis_size(axis)
    return lax.ppermute(value, axis, [(i, (i + steps) % count) for i in range(count)])


def local(adjoint_in, vertical, tiles, sources, lengths, prior):
    blocks, levels, width = adjoint_in.shape
    listed = tiles.shape[1]
    half = blocks // 2
    parts = 4
    flat = tiles.reshape((blocks * listed,) + tiles.shape[2:])
    rim = jax.ShapeDtypeStruct((half, levels, width), jnp.bfloat16)
    tile_scratch = pltpu.VMEM(flat.shape, flat.dtype)
    rim_running = pltpu.VMEM((blocks + 1, levels, width), jnp.float32)
    lists = [pltpu.SMEM((blocks * listed + GROUP,), jnp.int32)] * 2
    params = pltpu.CompilerParams(vmem_limit_bytes=VMEM_BYTES)
    cost = pl.CostEstimate(flops=400_000_000, bytes_accessed=8_000_000, transcendentals=0)

    low_a, up_a, lifted = pl.pallas_call(
        functools.partial(early_kernel, "col", (0, half), (half, blocks), parts),
        out_shape=[rim, rim, jax.ShapeDtypeStruct(adjoint_in.shape, jnp.bfloat16)],
        in_specs=[SMEM, SMEM, HBM, HBM, HBM],
        out_specs=[VMEM, VMEM, VMEM],
        scratch_shapes=[
            pltpu.VMEM(adjoint_in.shape, adjoint_in.dtype),
            pltpu.VMEM(vertical.shape, vertical.dtype),
            tile_scratch,
            rim_running,
            *lists,
            pltpu.SemaphoreType.DMA((2,)),
            pltpu.SemaphoreType.DMA((parts,)),
        ],
        compiler_params=params,
        cost_estimate=cost,
        name="early",
    )(sources, lengths, adjoint_in, vertical, flat)
    got_low_a = shift(low_a, "col", -1)
    got_up_a = shift(up_a, "col", 1)
    low_b, up_b = pl.pallas_call(
        functools.partial(late_kernel, "col", (half, blocks), (0, half), parts),
        out_shape=[rim, rim],
        in_specs=[SMEM, SMEM, VMEM, HBM],
        out_specs=[VMEM, VMEM],
        scratch_shapes=[tile_scratch, rim_running, *lists, pltpu.SemaphoreType.DMA((parts,))],
        compiler_params=params,
        cost_estimate=cost,
        name="late",
    )(sources, lengths, lifted, flat)
    got_low_b = shift(low_b, "col", -1)
    got_up_b = shift(up_b, "col", 1)
    partial = pl.pallas_call(
        functools.partial(middle_kernel, "col", parts, 0, half),
        out_shape=jax.ShapeDtypeStruct(prior.shape, prior.dtype),
        in_specs=[SMEM, SMEM, VMEM, HBM, HBM, HBM, HBM],
        out_specs=HBM,
        scratch_shapes=[
            tile_scratch,
            rim_running,
            pltpu.VMEM(rim.shape, rim.dtype),
            pltpu.VMEM(rim.shape, rim.dtype),
            *lists,
            pltpu.SemaphoreType.DMA((4,)),
            pltpu.SemaphoreType.DMA((parts,)),
        ],
        compiler_params=params,
        cost_estimate=cost,
        name="middle",
    )(sources, lengths, lifted, flat, prior, got_low_a, got_up_a)
    return partial + jnp.concatenate([got_up_b, got_low_b]).astype(jnp.float32)


def solution(mesh):
    placed = (
        P(("grp", "col"), None, None),
        P(("grp", "col"), None, None),
        P(("grp", "col"), None, None, None),
        P(("grp", "col"), None),
        P(("grp", "col")),
        P(("grp", "col"), None, None),
    )
    return jax.shard_map(
        local, mesh=mesh, in_specs=placed, out_specs=P(("grp", "col"), None, None), check_vma=False
    )
```

```python
import functools

import jax
import jax.numpy as jnp
from jax import lax
from jax.experimental import pallas as pl
from jax.experimental.pallas import tpu as pltpu
from jax.sharding import PartitionSpec as P

GROUP = 8
UNROLL = 4
FIRST = 16
VMEM_BYTES = 48 << 20


def relative(source, first, blocks, everywhere):
    rel = source - first
    rel = jnp.where(rel < -blocks, rel + everywhere, rel)
    return jnp.where(rel >= 2 * blocks, rel - everywhere, rel)


def list_entries(t, count, pick, first, everywhere, src_ref, len_ref, entry_list, row_list):
    listed, blocks = src_ref.shape
    length = len_ref[t]
    for k in range(listed):
        rel = relative(src_ref[k, t], first, blocks, everywhere)
        keep, row = pick(rel)
        keep = jnp.logical_and(keep, k < length)
        entry_list[count] = t * listed + k
        row_list[count] = row
        count = count + keep.astype(jnp.int32)
    return count


def close_list(count, zero_tile, entry_list, row_list, tiles):
    for extra in range(GROUP):
        entry_list[count + extra] = zero_tile
        row_list[count + extra] = 0
    tiles[zero_tile] = jnp.zeros_like(tiles[zero_tile])


def add_products(count, listed, width, entry_list, row_list, lifted, tiles, running):
    last = lifted.shape[0] - 1
    levels = lifted.shape[1]

    def group(g, carry):
        for u in range(GROUP):
            entry = entry_list[g * GROUP + u]
            row = row_list[g * GROUP + u]
            t = jnp.minimum(lax.div(entry, listed), last)
            product = jnp.dot(lifted[t], tiles[entry], preferred_element_type=jnp.float32)
            rows = pl.ds(row, levels, stride=width)
            running[rows, :] = running[rows, :] + product
        return carry

    lax.fori_loop(0, lax.div(count + (GROUP - 1), GROUP), group, 0)


def fetch_tiles(tiles_hbm, tiles, sems, parts):
    each = tiles_hbm.shape[0] // parts
    copies = []
    for part in range(parts):
        rows = pl.ds(part * each, each)
        copies.append(pltpu.make_async_copy(tiles_hbm.at[rows], tiles.at[rows], sems.at[part]))
    return copies


def pick_rim(blocks, low_from, up_from, width, up_base, rel):
    low = rel + (blocks - low_from)
    up = rel - (blocks + up_from)
    is_low = jnp.logical_and(low >= 0, low < width)
    is_up = jnp.logical_and(up >= 0, up < width)
    return jnp.logical_or(is_low, is_up), jnp.where(is_low, low, up + up_base)


def here(axis, blocks):
    return lax.axis_index(axis) * blocks, lax.axis_size(axis) * blocks


def emit(running, up_base, low_ref, up_ref):
    rows = low_ref.shape[0]
    low_ref[...] = running[:rows].astype(low_ref.dtype)
    up_ref[...] = running[up_base : up_base + rows].astype(up_ref.dtype)


def early_kernel(axis, low_from, up_from, width, parts, src_ref, len_ref, a, v, tiles_hbm, low_ref, up_ref, lifted,
                 tiles, running, entry_list, row_list, tile_sems):
    listed, blocks = src_ref.shape
    up_base = running.shape[0] // 2
    first, everywhere = here(axis, blocks)
    copies = fetch_tiles(tiles_hbm, tiles, tile_sems, parts)
    for copy in copies:
        copy.start()
    running[...] = jnp.zeros_like(running)
    pick = functools.partial(pick_rim, blocks, low_from, up_from, width, up_base)

    def lift(i, count):
        for u in range(UNROLL):
            t = i * UNROLL + u
            lifted[t] = lax.dot_general(
                v[t], a[t], (((0,), (0,)), ((), ())), preferred_element_type=jnp.float32
            ).astype(lifted.dtype)
            count = list_entries(t, count, pick, first, everywhere, src_ref, len_ref, entry_list, row_list)
        return count

    count = lax.fori_loop(0, blocks // UNROLL, lift, jnp.int32(0))
    close_list(count, blocks * listed, entry_list, row_list, tiles)
    for copy in copies:
        copy.wait()
    add_products(count, listed, width, entry_list, row_list, lifted, tiles, running)
    emit(running, up_base, low_ref, up_ref)


def late_kernel(axis, low_from, up_from, width, parts, src_ref, len_ref, lifted, tiles_hbm, low_ref, up_ref,
                tiles, running, entry_list, row_list, tile_sems):
    listed, blocks = src_ref.shape
    up_base = running.shape[0] // 2
    first, everywhere = here(axis, blocks)
    copies = fetch_tiles(tiles_hbm, tiles, tile_sems, parts)
    for copy in copies:
        copy.start()
    running[...] = jnp.zeros_like(running)
    pick = functools.partial(pick_rim, blocks, low_from, up_from, width, up_base)
    visit = lambda t, count: list_entries(t, count, pick, first, everywhere, src_ref, len_ref, entry_list, row_list)
    count = lax.fori_loop(0, blocks, visit, jnp.int32(0))
    close_list(count, blocks * listed, entry_list, row_list, tiles)
    for copy in copies:
        copy.wait()
    add_products(count, listed, width, entry_list, row_list, lifted, tiles, running)
    emit(running, up_base, low_ref, up_ref)


def middle_kernel(axis, parts, src_ref, len_ref, lifted, tiles_hbm, prior_hbm, running,
                  tiles, entry_list, row_list, prior_sem, tile_sems):
    listed, blocks = src_ref.shape
    first, everywhere = here(axis, blocks)
    copy_prior = pltpu.make_async_copy(prior_hbm, running, prior_sem)
    copy_prior.start()
    copies = fetch_tiles(tiles_hbm, tiles, tile_sems, parts)
    for copy in copies:
        copy.start()

    def pick(rel):
        return jnp.logical_and(rel >= 0, rel < blocks), rel

    visit = lambda t, count: list_entries(t, count, pick, first, everywhere, src_ref, len_ref, entry_list, row_list)
    count = lax.fori_loop(0, blocks, visit, jnp.int32(0))
    close_list(count, blocks * listed, entry_list, row_list, tiles)
    copy_prior.wait()
    for copy in copies:
        copy.wait()
    add_products(count, listed, blocks, entry_list, row_list, lifted, tiles, running)


SMEM = pl.BlockSpec(memory_space=pltpu.SMEM)
VMEM = pl.BlockSpec(memory_space=pltpu.VMEM)
HBM = pl.BlockSpec(memory_space=pl.ANY)


def shift(value, axis, steps):
    count = lax.axis_size(axis)
    return lax.ppermute(value, axis, [(i, (i + steps) % count) for i in range(count)])


def local(adjoint_in, vertical, tiles, sources, lengths, prior):
    blocks, levels, width = adjoint_in.shape
    listed = tiles.shape[1]
    wide = min(blocks, FIRST)
    thin = blocks - wide
    parts = 4
    flat = tiles.reshape((blocks * listed,) + tiles.shape[2:])
    by_entry = sources.T
    prior_rows = prior.transpose(1, 0, 2).reshape(levels * blocks, width)
    tile_scratch = pltpu.VMEM((blocks * listed + 1,) + flat.shape[1:], flat.dtype)
    lists = [pltpu.SMEM((blocks * listed + GROUP,), jnp.int32)] * 2
    params = pltpu.CompilerParams(vmem_limit_bytes=VMEM_BYTES)
    cost = pl.CostEstimate(flops=400_000_000, bytes_accessed=8_000_000, transcendentals=0)

    def rim(count):
        return jax.ShapeDtypeStruct((levels * count, width), jnp.bfloat16)

    def rim_running(count):
        return pltpu.VMEM((2 * (-(-levels * count // 16) * 16), width), jnp.float32)

    low_a, up_a, lifted = pl.pallas_call(
        functools.partial(early_kernel, "col", 0, thin, wide, parts),
        out_shape=[rim(wide), rim(wide), jax.ShapeDtypeStruct(adjoint_in.shape, jnp.bfloat16)],
        in_specs=[SMEM, SMEM, VMEM, VMEM, HBM],
        out_specs=[VMEM, VMEM, VMEM],
        scratch_shapes=[tile_scratch, rim_running(wide), *lists, pltpu.SemaphoreType.DMA((parts,))],
        compiler_params=params,
        cost_estimate=cost,
        name="early",
    )(by_entry, lengths, adjoint_in, vertical, flat)
    low_a = shift(low_a, "col", -1)
    up_a = shift(up_a, "col", 1)
    low_b, up_b = pl.pallas_call(
        functools.partial(late_kernel, "col", wide, 0, thin, parts),
        out_shape=[rim(thin), rim(thin)],
        in_specs=[SMEM, SMEM, VMEM, HBM],
        out_specs=[VMEM, VMEM],
        scratch_shapes=[tile_scratch, rim_running(thin), *lists, pltpu.SemaphoreType.DMA((parts,))],
        compiler_params=params,
        cost_estimate=cost,
        name="late",
    )(by_entry, lengths, lifted, flat)
    low_b = shift(low_b, "col", -1)
    up_b = shift(up_b, "col", 1)
    middle = pl.pallas_call(
        functools.partial(middle_kernel, "col", parts),
        out_shape=jax.ShapeDtypeStruct(prior_rows.shape, prior.dtype),
        in_specs=[SMEM, SMEM, VMEM, HBM, HBM],
        out_specs=VMEM,
        scratch_shapes=[tile_scratch, *lists, pltpu.SemaphoreType.DMA, pltpu.SemaphoreType.DMA((parts,))],
        compiler_params=params,
        cost_estimate=cost,
        name="middle",
    )(by_entry, lengths, lifted, flat, prior_rows)

    def joined(left, right):
        pieces = [piece.reshape(levels, -1, width) for piece in (left, right)]
        return jnp.concatenate(pieces, axis=1).astype(jnp.float32)

    total = middle.reshape(levels, blocks, width) + joined(low_a, low_b) + joined(up_b, up_a)
    return total.transpose(1, 0, 2)


def solution(mesh):
    placed = (
        P(("grp", "col"), None, None),
        P(("grp", "col"), None, None),
        P(("grp", "col"), None, None, None),
        P(("grp", "col"), None),
        P(("grp", "col")),
        P(("grp", "col"), None, None),
    )
    return jax.shard_map(
        local, mesh=mesh, in_specs=placed, out_specs=P(("grp", "col"), None, None), check_vma=False
    )
```

```python
import functools

import jax
import jax.numpy as jnp
from jax import lax
from jax.experimental import pallas as pl
from jax.experimental.pallas import tpu as pltpu
from jax.sharding import PartitionSpec as P

GROUP = 8
UNROLL = 4
FIRST = 16
VMEM_BYTES = 48 << 20


def relative(source, first, blocks, everywhere):
    rel = source - first
    rel = jnp.where(rel < -blocks, rel + everywhere, rel)
    return jnp.where(rel >= 2 * blocks, rel - everywhere, rel)


def list_entries(t, count, pick, first, everywhere, src_ref, len_ref, entry_list, row_list):
    listed, blocks = src_ref.shape
    length = len_ref[t]
    for k in range(listed):
        rel = relative(src_ref[k, t], first, blocks, everywhere)
        keep, row = pick(rel)
        keep = jnp.logical_and(keep, k < length)
        entry_list[count] = t * listed + k
        row_list[count] = row
        count = count + keep.astype(jnp.int32)
    return count


def close_list(count, zero_tile, entry_list, row_list, tiles):
    for extra in range(GROUP):
        entry_list[count + extra] = zero_tile
        row_list[count + extra] = 0
    tiles[zero_tile] = jnp.zeros_like(tiles[zero_tile])


def add_products(count, listed, stride, entry_list, row_list, lifted, tiles, running):
    last = lifted.shape[0] - 1
    levels = lifted.shape[1]

    def group(g, carry):
        for u in range(GROUP):
            entry = entry_list[g * GROUP + u]
            row = row_list[g * GROUP + u]
            t = jnp.minimum(lax.div(entry, listed), last)
            product = jnp.dot(lifted[t], tiles[entry], preferred_element_type=jnp.float32)
            rows = pl.ds(row, levels, stride=stride)
            running[rows, :] = running[rows, :] + product
        return carry

    lax.fori_loop(0, lax.div(count + (GROUP - 1), GROUP), group, 0)


def fetch_tiles(tiles_hbm, tiles, sems, parts):
    each = tiles_hbm.shape[0] // parts
    copies = []
    for part in range(parts):
        rows = pl.ds(part * each, each)
        copies.append(pltpu.make_async_copy(tiles_hbm.at[rows], tiles.at[rows], sems.at[part]))
    return copies


def pick_rim(blocks, low_from, up_from, width, up_base, rel):
    low = rel + (blocks - low_from)
    up = rel - (blocks + up_from)
    is_low = jnp.logical_and(low >= 0, low < width)
    is_up = jnp.logical_and(up >= 0, up < width)
    return jnp.logical_or(is_low, is_up), jnp.where(is_low, low, up + up_base)


def here(axis, blocks):
    return lax.axis_index(axis) * blocks, lax.axis_size(axis) * blocks


def emit(running, up_base, stride, width, low_ref, up_ref):
    lanes = running.shape[1]
    for base, ref in ((0, low_ref), (up_base, up_ref)):
        levels = ref.shape[0] // width
        rows = running[base : base + levels * stride].reshape(levels, stride, lanes)
        ref[...] = rows[:, :width].reshape(levels * width, lanes).astype(ref.dtype)


def early_kernel(axis, low_from, up_from, width, stride, parts, src_ref, len_ref, a, v, tiles_hbm, low_ref, up_ref, lifted,
                 tiles, running, entry_list, row_list, tile_sems):
    listed, blocks = src_ref.shape
    up_base = running.shape[0] // 2
    first, everywhere = here(axis, blocks)
    copies = fetch_tiles(tiles_hbm, tiles, tile_sems, parts)
    for copy in copies:
        copy.start()
    running[...] = jnp.zeros_like(running)
    pick = functools.partial(pick_rim, blocks, low_from, up_from, width, up_base)

    def lift(i, count):
        for u in range(UNROLL):
            t = i * UNROLL + u
            lifted[t] = lax.dot_general(
                v[t], a[t], (((0,), (0,)), ((), ())), preferred_element_type=jnp.float32
            ).astype(lifted.dtype)
            count = list_entries(t, count, pick, first, everywhere, src_ref, len_ref, entry_list, row_list)
        return count

    count = lax.fori_loop(0, blocks // UNROLL, lift, jnp.int32(0))
    close_list(count, blocks * listed, entry_list, row_list, tiles)
    for copy in copies:
        copy.wait()
    add_products(count, listed, stride, entry_list, row_list, lifted, tiles, running)
    emit(running, up_base, stride, width, low_ref, up_ref)


def late_kernel(axis, low_from, up_from, width, stride, parts, src_ref, len_ref, lifted, tiles_hbm, low_ref, up_ref,
                tiles, running, entry_list, row_list, tile_sems):
    listed, blocks = src_ref.shape
    up_base = running.shape[0] // 2
    first, everywhere = here(axis, blocks)
    copies = fetch_tiles(tiles_hbm, tiles, tile_sems, parts)
    for copy in copies:
        copy.start()
    running[...] = jnp.zeros_like(running)
    pick = functools.partial(pick_rim, blocks, low_from, up_from, width, up_base)
    visit = lambda t, count: list_entries(t, count, pick, first, everywhere, src_ref, len_ref, entry_list, row_list)
    count = lax.fori_loop(0, blocks, visit, jnp.int32(0))
    close_list(count, blocks * listed, entry_list, row_list, tiles)
    for copy in copies:
        copy.wait()
    add_products(count, listed, stride, entry_list, row_list, lifted, tiles, running)
    emit(running, up_base, stride, width, low_ref, up_ref)


def middle_kernel(axis, parts, src_ref, len_ref, lifted, tiles_hbm, prior_hbm, running,
                  tiles, entry_list, row_list, prior_sem, tile_sems):
    listed, blocks = src_ref.shape
    first, everywhere = here(axis, blocks)
    copy_prior = pltpu.make_async_copy(prior_hbm, running, prior_sem)
    copy_prior.start()
    copies = fetch_tiles(tiles_hbm, tiles, tile_sems, parts)
    for copy in copies:
        copy.start()

    def pick(rel):
        return jnp.logical_and(rel >= 0, rel < blocks), rel

    visit = lambda t, count: list_entries(t, count, pick, first, everywhere, src_ref, len_ref, entry_list, row_list)
    count = lax.fori_loop(0, blocks, visit, jnp.int32(0))
    close_list(count, blocks * listed, entry_list, row_list, tiles)
    copy_prior.wait()
    for copy in copies:
        copy.wait()
    add_products(count, listed, blocks, entry_list, row_list, lifted, tiles, running)


SMEM = pl.BlockSpec(memory_space=pltpu.SMEM)
VMEM = pl.BlockSpec(memory_space=pltpu.VMEM)
HBM = pl.BlockSpec(memory_space=pl.ANY)


def shift(value, axis, steps):
    count = lax.axis_size(axis)
    return lax.ppermute(value, axis, [(i, (i + steps) % count) for i in range(count)])


def local(adjoint_in, vertical, tiles, sources, lengths, prior):
    blocks, levels, width = adjoint_in.shape
    listed = tiles.shape[1]
    wide = min(blocks, FIRST)
    thin = blocks - wide
    parts = 4
    flat = tiles.reshape((blocks * listed,) + tiles.shape[2:])
    by_entry = sources.T
    prior_rows = prior.transpose(1, 0, 2).reshape(levels * blocks, width)
    tile_scratch = pltpu.VMEM((blocks * listed + 1,) + flat.shape[1:], flat.dtype)
    lists = [pltpu.SMEM((blocks * listed + GROUP,), jnp.int32)] * 2
    params = pltpu.CompilerParams(vmem_limit_bytes=VMEM_BYTES)
    cost = pl.CostEstimate(flops=400_000_000, bytes_accessed=8_000_000, transcendentals=0)

    def rim(count):
        return jax.ShapeDtypeStruct((levels * count, width), jnp.bfloat16)

    def rim_running(count):
        return pltpu.VMEM((2 * (-(-levels * count // 16) * 16), width), jnp.float32)

    low_a, up_a, lifted = pl.pallas_call(
        functools.partial(early_kernel, "col", 0, thin, wide, blocks, parts),
        out_shape=[rim(wide), rim(wide), jax.ShapeDtypeStruct(adjoint_in.shape, jnp.bfloat16)],
        in_specs=[SMEM, SMEM, VMEM, VMEM, HBM],
        out_specs=[VMEM, VMEM, VMEM],
        scratch_shapes=[tile_scratch, rim_running(blocks), *lists, pltpu.SemaphoreType.DMA((parts,))],
        compiler_params=params,
        cost_estimate=cost,
        name="early",
    )(by_entry, lengths, adjoint_in, vertical, flat)
    low_a = shift(low_a, "col", -1)
    up_a = shift(up_a, "col", 1)
    low_b, up_b = pl.pallas_call(
        functools.partial(late_kernel, "col", wide, 0, thin, thin, parts),
        out_shape=[rim(thin), rim(thin)],
        in_specs=[SMEM, SMEM, VMEM, HBM],
        out_specs=[VMEM, VMEM],
        scratch_shapes=[tile_scratch, rim_running(thin), *lists, pltpu.SemaphoreType.DMA((parts,))],
        compiler_params=params,
        cost_estimate=cost,
        name="late",
    )(by_entry, lengths, lifted, flat)
    low_b = shift(low_b, "col", -1)
    up_b = shift(up_b, "col", 1)
    middle = pl.pallas_call(
        functools.partial(middle_kernel, "col", parts),
        out_shape=jax.ShapeDtypeStruct(prior_rows.shape, prior.dtype),
        in_specs=[SMEM, SMEM, VMEM, HBM, HBM],
        out_specs=VMEM,
        scratch_shapes=[tile_scratch, *lists, pltpu.SemaphoreType.DMA, pltpu.SemaphoreType.DMA((parts,))],
        compiler_params=params,
        cost_estimate=cost,
        name="middle",
    )(by_entry, lengths, lifted, flat, prior_rows)

    def joined(left, right):
        pieces = [piece.reshape(levels, -1, width) for piece in (left, right)]
        return jnp.concatenate(pieces, axis=1).astype(jnp.float32)

    total = middle.reshape(levels, blocks, width) + joined(low_a, low_b) + joined(up_b, up_a)
    return total.transpose(1, 0, 2)


def solution(mesh):
    placed = (
        P(("grp", "col"), None, None),
        P(("grp", "col"), None, None),
        P(("grp", "col"), None, None, None),
        P(("grp", "col"), None),
        P(("grp", "col")),
        P(("grp", "col"), None, None),
    )
    return jax.shard_map(
        local, mesh=mesh, in_specs=placed, out_specs=P(("grp", "col"), None, None), check_vma=False
    )
```

```python
import functools

import jax
import jax.numpy as jnp
from jax import lax
from jax.experimental import pallas as pl
from jax.experimental.pallas import tpu as pltpu
from jax.sharding import PartitionSpec as P

GROUP = 8
UNROLL = 8
FIRST = 16
VMEM_BYTES = 48 << 20


def relative(source, first, blocks, everywhere):
    rel = source - first
    rel = jnp.where(rel < -blocks, rel + everywhere, rel)
    return jnp.where(rel >= 2 * blocks, rel - everywhere, rel)


def list_entries(t, count, pick, first, everywhere, src_ref, len_ref, entry_list, row_list):
    listed, blocks = src_ref.shape
    length = len_ref[t]
    for k in range(listed):
        rel = relative(src_ref[k, t], first, blocks, everywhere)
        keep, row = pick(rel)
        keep = jnp.logical_and(keep, k < length)
        entry_list[count] = t * listed + k
        row_list[count] = row
        count = count + keep.astype(jnp.int32)
    return count


def close_list(count, zero_tile, entry_list, row_list, tiles):
    for extra in range(GROUP):
        entry_list[count + extra] = zero_tile
        row_list[count + extra] = 0
    tiles[zero_tile] = jnp.zeros_like(tiles[zero_tile])


def add_products(count, listed, stride, entry_list, row_list, lifted, tiles, running):
    last = lifted.shape[0] - 1
    levels = lifted.shape[1]

    def group(g, carry):
        for u in range(GROUP):
            entry = entry_list[g * GROUP + u]
            row = row_list[g * GROUP + u]
            t = jnp.minimum(lax.div(entry, listed), last)
            product = jnp.dot(lifted[t], tiles[entry], preferred_element_type=jnp.float32)
            rows = pl.ds(row, levels, stride=stride)
            running[rows, :] = running[rows, :] + product
        return carry

    lax.fori_loop(0, lax.div(count + (GROUP - 1), GROUP), group, 0)


def fetch_tiles(tiles_hbm, tiles, sems, parts):
    each = tiles_hbm.shape[0] // parts
    copies = []
    for part in range(parts):
        rows = pl.ds(part * each, each)
        copies.append(pltpu.make_async_copy(tiles_hbm.at[rows], tiles.at[rows], sems.at[part]))
    return copies


def pick_rim(blocks, low_from, up_from, width, up_base, rel):
    low = rel + (blocks - low_from)
    up = rel - (blocks + up_from)
    is_low = jnp.logical_and(low >= 0, low < width)
    is_up = jnp.logical_and(up >= 0, up < width)
    return jnp.logical_or(is_low, is_up), jnp.where(is_low, low, up + up_base)


def here(axis, blocks):
    return lax.axis_index(axis) * blocks, lax.axis_size(axis) * blocks


def emit(running, up_base, stride, width, low_ref, up_ref):
    lanes = running.shape[1]
    for base, ref in ((0, low_ref), (up_base, up_ref)):
        levels = ref.shape[0] // width
        rows = running[base : base + levels * stride].reshape(levels, stride, lanes)
        ref[...] = rows[:, :width].reshape(levels * width, lanes).astype(ref.dtype)


def early_kernel(axis, low_from, up_from, width, stride, parts, src_ref, len_ref, a, v, tiles_hbm, low_ref, up_ref, lifted,
                 tiles, running, entry_list, row_list, tile_sems):
    listed, blocks = src_ref.shape
    up_base = running.shape[0] // 2
    first, everywhere = here(axis, blocks)
    copies = fetch_tiles(tiles_hbm, tiles, tile_sems, parts)
    for copy in copies:
        copy.start()
    running[...] = jnp.zeros_like(running)
    pick = functools.partial(pick_rim, blocks, low_from, up_from, width, up_base)

    def lift(i, count):
        for u in range(UNROLL):
            t = i * UNROLL + u
            lifted[t] = lax.dot_general(
                v[t], a[t], (((0,), (0,)), ((), ())), preferred_element_type=jnp.float32
            ).astype(lifted.dtype)
            count = list_entries(t, count, pick, first, everywhere, src_ref, len_ref, entry_list, row_list)
        return count

    count = lax.fori_loop(0, blocks // UNROLL, lift, jnp.int32(0))
    close_list(count, blocks * listed, entry_list, row_list, tiles)
    for copy in copies:
        copy.wait()
    add_products(count, listed, stride, entry_list, row_list, lifted, tiles, running)
    emit(running, up_base, stride, width, low_ref, up_ref)


def late_kernel(axis, low_from, up_from, width, stride, parts, src_ref, len_ref, lifted, tiles_hbm, low_ref, up_ref,
                tiles, running, entry_list, row_list, tile_sems):
    listed, blocks = src_ref.shape
    up_base = running.shape[0] // 2
    first, everywhere = here(axis, blocks)
    copies = fetch_tiles(tiles_hbm, tiles, tile_sems, parts)
    for copy in copies:
        copy.start()
    running[...] = jnp.zeros_like(running)
    pick = functools.partial(pick_rim, blocks, low_from, up_from, width, up_base)
    visit = lambda t, count: list_entries(t, count, pick, first, everywhere, src_ref, len_ref, entry_list, row_list)
    count = lax.fori_loop(0, blocks, visit, jnp.int32(0))
    close_list(count, blocks * listed, entry_list, row_list, tiles)
    for copy in copies:
        copy.wait()
    add_products(count, listed, stride, entry_list, row_list, lifted, tiles, running)
    emit(running, up_base, stride, width, low_ref, up_ref)


def middle_kernel(axis, parts, src_ref, len_ref, lifted, tiles_hbm, prior_hbm, running,
                  tiles, entry_list, row_list, prior_sem, tile_sems):
    listed, blocks = src_ref.shape
    first, everywhere = here(axis, blocks)
    copy_prior = pltpu.make_async_copy(prior_hbm, running, prior_sem)
    copy_prior.start()
    copies = fetch_tiles(tiles_hbm, tiles, tile_sems, parts)
    for copy in copies:
        copy.start()

    def pick(rel):
        return jnp.logical_and(rel >= 0, rel < blocks), rel

    visit = lambda t, count: list_entries(t, count, pick, first, everywhere, src_ref, len_ref, entry_list, row_list)
    count = lax.fori_loop(0, blocks, visit, jnp.int32(0))
    close_list(count, blocks * listed, entry_list, row_list, tiles)
    copy_prior.wait()
    for copy in copies:
        copy.wait()
    add_products(count, listed, blocks, entry_list, row_list, lifted, tiles, running)


SMEM = pl.BlockSpec(memory_space=pltpu.SMEM)
VMEM = pl.BlockSpec(memory_space=pltpu.VMEM)
HBM = pl.BlockSpec(memory_space=pl.ANY)


def shift(value, axis, steps):
    count = lax.axis_size(axis)
    return lax.ppermute(value, axis, [(i, (i + steps) % count) for i in range(count)])


def local(adjoint_in, vertical, tiles, sources, lengths, prior):
    blocks, levels, width = adjoint_in.shape
    listed = tiles.shape[1]
    wide = min(blocks, FIRST)
    thin = blocks - wide
    parts = 4
    flat = tiles.reshape((blocks * listed,) + tiles.shape[2:])
    by_entry = sources.T
    prior_rows = prior.transpose(1, 0, 2).reshape(levels * blocks, width)
    tile_scratch = pltpu.VMEM((blocks * listed + 1,) + flat.shape[1:], flat.dtype)
    lists = [pltpu.SMEM((blocks * listed + GROUP,), jnp.int32)] * 2
    params = pltpu.CompilerParams(vmem_limit_bytes=VMEM_BYTES)
    cost = pl.CostEstimate(flops=400_000_000, bytes_accessed=8_000_000, transcendentals=0)

    def rim(count):
        return jax.ShapeDtypeStruct((levels * count, width), jnp.bfloat16)

    def rim_running(count):
        return pltpu.VMEM((2 * (-(-levels * count // 16) * 16), width), jnp.float32)

    low_a, up_a, lifted = pl.pallas_call(
        functools.partial(early_kernel, "col", 0, thin, wide, blocks, parts),
        out_shape=[rim(wide), rim(wide), jax.ShapeDtypeStruct(adjoint_in.shape, jnp.bfloat16)],
        in_specs=[SMEM, SMEM, VMEM, VMEM, HBM],
        out_specs=[VMEM, VMEM, VMEM],
        scratch_shapes=[tile_scratch, rim_running(blocks), *lists, pltpu.SemaphoreType.DMA((parts,))],
        compiler_params=params,
        cost_estimate=cost,
        name="early",
    )(by_entry, lengths, adjoint_in, vertical, flat)
    low_a = shift(low_a, "col", -1)
    up_a = shift(up_a, "col", 1)
    low_b, up_b = pl.pallas_call(
        functools.partial(late_kernel, "col", wide, 0, thin, thin, parts),
        out_shape=[rim(thin), rim(thin)],
        in_specs=[SMEM, SMEM, VMEM, HBM],
        out_specs=[VMEM, VMEM],
        scratch_shapes=[tile_scratch, rim_running(thin), *lists, pltpu.SemaphoreType.DMA((parts,))],
        compiler_params=params,
        cost_estimate=cost,
        name="late",
    )(by_entry, lengths, lifted, flat)
    low_b = shift(low_b, "col", -1)
    up_b = shift(up_b, "col", 1)
    middle = pl.pallas_call(
        functools.partial(middle_kernel, "col", parts),
        out_shape=jax.ShapeDtypeStruct(prior_rows.shape, prior.dtype),
        in_specs=[SMEM, SMEM, VMEM, HBM, HBM],
        out_specs=VMEM,
        scratch_shapes=[tile_scratch, *lists, pltpu.SemaphoreType.DMA, pltpu.SemaphoreType.DMA((parts,))],
        compiler_params=params,
        cost_estimate=cost,
        name="middle",
    )(by_entry, lengths, lifted, flat, prior_rows)

    def joined(left, right):
        pieces = [piece.reshape(levels, -1, width) for piece in (left, right)]
        return jnp.concatenate(pieces, axis=1).astype(jnp.float32)

    total = middle.reshape(levels, blocks, width) + joined(low_a, low_b) + joined(up_b, up_a)
    return total.transpose(1, 0, 2)


def solution(mesh):
    placed = (
        P(("grp", "col"), None, None),
        P(("grp", "col"), None, None),
        P(("grp", "col"), None, None, None),
        P(("grp", "col"), None),
        P(("grp", "col")),
        P(("grp", "col"), None, None),
    )
    return jax.shard_map(
        local, mesh=mesh, in_specs=placed, out_specs=P(("grp", "col"), None, None), check_vma=False
    )
```
